256 devices in a mesh: row: 32 (over y, z), col: 8 (over x, core).
Axes of the slice: x: 4, y: 4, z: 8, core: 2. Of those that a mesh axis runs over, the one named last changes fastest.
Arguments:
- matrix: float32 [1, 32, 512, 4, 8, 512], P(None, 'row', None, None, 'col'), may hold values from -6 to 6
- pivots: int32 [2, 512], replicated, may hold values from 0 to 16383, as said below
- inverses: float32 [2, 512, 512], replicated, may hold values from -0.01171875 to 0.01171875
Outputs:
- factored: float32 [1, 32, 512, 4, 8, 512], P(None, 'row', None, None, 'col')
The draws below stay inside these ranges and needn't reach their ends.
Inputs may be any that keep to these rules, and one draw needn't show every extreme that they name: pivots[k, t] is either 512 * k + t itself or a row at or after 512 * (k + 1); the entries of one panel's list are distinct; position 0 of each panel keeps its own row, position 1 takes row 16383 and position 2 takes row 512 * (k + 1).
All inputs are finite; a program needn't handle non-finite values.
Results may differ from the reference program's by a relative error of at most 0.00011.
Values sent between devices are 32-bit elements; how exact they have to be, the bound alone decides.
No kernel may reach another device: no remote copies, remote signals or barrier semaphores. Data moves between devices by JAX's collectives and lax.ppermute only.
A program may use at most 128 MiB of HBM per device.

```python
import jax
import jax.numpy as jnp
from jax import lax

N = 16384
NB = 512
PANELS = 2
N_ROW = 32
N_COL = 8


def draw_pivots(key, part):
    key = jax.random.fold_in(key, 7)
    lists = []
    for panel in range(PANELS):
        sub_key = jax.random.fold_in(key, panel)
        first = (panel + 1) * NB
        order = jax.random.permutation(jax.random.fold_in(sub_key, 1), N - first - 2).astype(jnp.int32) + first + 1
        stays = jax.random.randint(jax.random.fold_in(sub_key, 2), (NB,), 0, 8) == 0
        stays = stays.at[0].set(True).at[1].set(False).at[2].set(False)
        order = order[:NB].at[1].set(N - 1).at[2].set(first)
        own = panel * NB + jnp.arange(NB, dtype=jnp.int32)
        lists.append(jnp.where(stays, own, order))
    return jnp.stack(lists)


def level_of(rng, shape, pieces, low, high):
    loudness = 1.0
    for dim, shards_of in pieces:
        draws = jax.random.uniform(jax.random.fold_in(jax.random.fold_in(rng, 6), dim), (shards_of,), jnp.float32, low / len(pieces), high / len(pieces))
        loudness = loudness * jnp.repeat(jnp.exp(draws), shape[dim] // shards_of).reshape((-1,) + (1,) * (len(shape) - 1 - dim))
    return loudness


def gaussian(rng, shape, width, bound, split=(), kind=jnp.bfloat16):
    array = width * jax.random.normal(rng, shape, jnp.float32)
    if split:
        array = array * level_of(rng, shape, split, -0.22, 0.18)
    return jnp.clip(array, -bound, bound).astype(kind)


def setup_inputs(seed: int = 0) -> dict:
    key_list = jax.random.split(jax.random.key(seed), 4)
    return {
        "matrix": gaussian(key_list[0], (N // (NB * N_ROW), N_ROW, NB, N // (NB * N_COL), N_COL, NB), 1.0, 6.0, ((1, 32), (4, 8)), jnp.float32),
        "pivots": draw_pivots(jax.random.fold_in(key_list[3], 71), 0),
        "inverses": gaussian(key_list[2], (PANELS, NB, NB), (NB * NB) ** -0.5, 0.01171875, (), jnp.float32),
    }


def reference(matrix, pivots, inverses):
    full = matrix.reshape(N, N)
    for panel in range(PANELS):
        first_row = panel * NB
        after_row = first_row + NB
        positions = jnp.arange(N, dtype=jnp.int32)
        own = first_row + jnp.arange(NB, dtype=jnp.int32)
        source = positions.at[own].set(pivots[panel]).at[pivots[panel]].set(own)
        full = full[source]
        l_cols = jnp.dot(full[after_row:, first_row:after_row], inverses[panel], precision=lax.Precision.HIGHEST)
        full = full.at[after_row:, first_row:after_row].set(l_cols)
        update = jnp.dot(l_cols, full[first_row:after_row, after_row:], precision=lax.Precision.HIGHEST)
        full = full.at[after_row:, after_row:].set(full[after_row:, after_row:] - update)
    return full.reshape(matrix.shape)
```

```python
import functools

import jax
import jax.numpy as jnp
from jax import lax
from jax.experimental import pallas as pl
from jax.experimental.pallas import tpu as pltpu
from jax.sharding import Mesh, PartitionSpec as P

Y, Z, X, CORE = 4, 8, 4, 2
NB = 512
LANES = 128
SUB = 16
SLOTS = 8
CAP = 4 * SLOTS
ROW = ("y", "z")
COL = ("x", "core")
HIGHEST = lax.Precision.HIGHEST
F32 = jnp.float32
I32 = jnp.int32


def from_root(x, axis, root):
    mine = lax.axis_index(axis) == root
    return lax.psum(jnp.where(mine, x, jnp.zeros_like(x)), axis)


def general(work, pivots, inverses):
    row_index = lax.axis_index(ROW)
    col_index = lax.axis_index(COL)
    work = work.reshape(NB, SUB * LANES)
    row_ids = row_index * NB + jnp.arange(NB, dtype=I32)
    col_ids = (
        (jnp.arange(4, dtype=I32)[:, None] * 8 + col_index) * NB
        + jnp.arange(NB, dtype=I32)[None, :]
    ).reshape(-1)
    for panel in range(2):
        after_row = (panel + 1) * NB
        targets = pivots[panel]
        held = targets // NB == row_index
        local_row = targets % NB
        picked = jnp.where(held[:, None], jnp.take(work, local_row, axis=0), 0.0)
        u_rows = lax.psum(picked, ROW)
        displaced = from_root(work, ROW, panel)
        dest_row = jnp.where(held, local_row, NB)
        work = work.at[dest_row].set(displaced, mode="drop")
        work = jnp.where(row_index == panel, u_rows, work)
        panel_cols = work[:, :NB]
        product = jnp.dot(panel_cols, inverses[panel], precision=HIGHEST)
        l_cols = from_root(product, COL, panel)
        below_mask = (row_ids >= after_row)[:, None]
        work = work.at[:, :NB].set(
            jnp.where(below_mask & (col_index == panel), l_cols, panel_cols)
        )
        update = jnp.dot(l_cols, u_rows, precision=HIGHEST)
        trail_mask = below_mask & (col_ids >= after_row)[None, :]
        work = jnp.where(trail_mask, work - update, work)
    return work.reshape(NB * SUB, LANES)


def ranks(key):
    t = jnp.arange(NB, dtype=I32)
    same = (key[:, None] == key[None, :]) & (t[None, :] < t[:, None])
    less = key[None, :] < key[:, None]
    rank = jnp.sum(same.astype(I32), axis=1)
    place = rank + jnp.sum(less.astype(I32), axis=1)
    return rank, place


def plan(pivots, y, z):
    r = y * Z + z
    t = jnp.arange(NB, dtype=I32)
    piv0, piv1 = pivots[0], pivots[1]
    meet = piv1[:, None] == piv0[None, :]
    src1 = jnp.where(jnp.any(meet, 1), jnp.sum(jnp.where(meet, t[None, :], 0), 1), piv1)
    src = (piv0, src1)
    in_home = piv0[:, None] == NB + t[None, :]
    moved = piv0[:, None] == piv1[None, :]
    dst0 = jnp.where(
        jnp.any(in_home, 1),
        jnp.sum(jnp.where(in_home, piv1[None, :], 0), 1),
        jnp.where(jnp.any(moved, 1), NB + jnp.sum(jnp.where(moved, t[None, :], 0), 1), piv0),
    )
    taken = (NB + t)[:, None] == piv0[None, :]
    dst1 = jnp.where(jnp.any(taken, 1), jnp.sum(jnp.where(taken, t[None, :], 0), 1), piv1)
    dst = (dst0, dst1)

    k_rank, k_place, k_key = [], [], []
    h_rank, h_place, h_key = [], [], []
    for h in range(2):
        own = h * NB + t
        stay = src[h] == own
        key = jnp.where(stay, -1, src[h] // NB)
        rank, place = ranks(key)
        k_key.append(key), k_rank.append(rank), k_place.append(place)
        away = dst[h] >= 2 * NB
        hkey = jnp.where(stay, -1, jnp.where(away, dst[h] // NB, 32))
        rank, place = ranks(hkey)
        h_key.append(hkey), h_rank.append(rank), h_place.append(place)
    over = jnp.zeros((), jnp.bool_)
    for h in range(2):
        over = over | jnp.any((k_key[h] >= 0) & (k_rank[h] >= CAP))
        over = over | jnp.any((h_key[h] >= 0) & (h_key[h] < 32) & (h_rank[h] >= CAP))

    def spot(place):
        return (place % 4) * 128 + place // 4

    mine = z % 2
    pick = lambda pair: jnp.where(mine == 0, pair[0], pair[1])
    home_spot = spot(pick(h_place))
    home_list = jnp.sum(jnp.where(home_spot[None, :] == t[:, None], t[None, :], 0), 1)
    e = jnp.arange(4 * SLOTS, dtype=I32)
    give = []
    for h in range(2):
        code = jnp.where(k_key[h] == r, (k_place[h] % 4) * SLOTS + k_rank[h] // 4, -1)
        code = jnp.where(k_rank[h] < CAP, code, -1)
        give.append(jnp.sum(jnp.where(code[None, :] == e[:, None], (src[h] % NB)[None, :], 0), 1))
    give_list = jnp.concatenate(give)
    place, key, rank = pick(k_place), pick(k_key), pick(k_rank)
    code = jnp.where(key < 0, -1, jnp.minimum(key * SLOTS + rank // 4, 32 * SLOTS - 1))
    i = jnp.arange(128, dtype=I32) * 4 + y
    slice_list = jnp.sum(jnp.where(place[None, :] == i[:, None], code[None, :], 0), 1)
    place, key, rank = pick(h_place), pick(h_key), pick(h_rank)
    ok = (place % 4 == y) & (key >= 0) & (key < 32) & (rank < CAP)
    code = jnp.where(ok, key * SLOTS + rank // 4, -1)
    e = jnp.arange(32 * SLOTS, dtype=I32)
    away_list = jnp.sum(jnp.where(code[None, :] == e[:, None], (place // 4)[None, :], 0), 1)
    e = jnp.arange(CAP, dtype=I32)
    to_row, from_y = [], []
    for h in range(2):
        hit = ((h_key[h] == r)[None, :]) & (h_rank[h][None, :] == e[:, None])
        to_row.append(jnp.sum(jnp.where(hit, (dst[h] % NB + 1)[None, :], 0), 1) - 1)
        from_y.append(jnp.sum(jnp.where(hit, (h_place[h] % 4)[None, :], 0), 1))
    to_row, from_y = jnp.concatenate(to_row), jnp.concatenate(from_y)
    hot = [(spot(k_place[h])[:, None] == t[None, :]).astype(F32) for h in range(2)]
    return home_list, give_list, slice_list, away_list, to_row, from_y, hot, over


def pack_kernel(home_ref, give_ref, x_ref, h_ref, g_ref):
    def home(n, _):
        row = home_ref[n] * SUB
        y, i = n // 128, n % 128
        for k in range(4):
            h_ref[pl.ds(((y * 4 + k) * 128 + i) * 4, 4), :] = x_ref[pl.ds(row + k, 4, stride=4), :]
        return 0

    def give(n, _):
        row = give_ref[n] * SUB
        h, y, s = n // (4 * SLOTS), (n // SLOTS) % 4, n % SLOTS
        for k in range(4):
            g_ref[pl.ds(((y * 8 + 2 * k + h) * SLOTS + s) * 4, 4), :] = x_ref[pl.ds(row + k, 4, stride=4), :]
        return 0

    lax.fori_loop(0, 8 * SLOTS, give, 0, unroll=4)
    lax.fori_loop(0, NB, home, 0, unroll=8)


def pack(home_list, give_list, x):
    return pl.pallas_call(
        pack_kernel,
        out_shape=[
            jax.ShapeDtypeStruct((NB * SUB, LANES), F32),
            jax.ShapeDtypeStruct((32 * SLOTS * 4, LANES), F32),
        ],
        in_specs=[pl.BlockSpec(memory_space=pltpu.SMEM)] * 2 + [pl.BlockSpec(memory_space=pltpu.VMEM)],
        out_specs=[pl.BlockSpec(memory_space=pltpu.VMEM)] * 2,
        compiler_params=pltpu.CompilerParams(vmem_limit_bytes=24 << 20),
        name="pack",
    )(home_list, give_list, x)


def slice_kernel(slice_ref, away_ref, hs_ref, recv_ref, s_ref, d_ref):
    def one(i, _):
        code = slice_ref[i]
        theirs = recv_ref[pl.ds(jnp.maximum(code, 0) * 4, 4), :]
        s_ref[pl.ds(i, 4, stride=128), :] = jnp.where(code < 0, hs_ref[pl.ds(i * 4, 4), :], theirs)
        return 0

    def away(n, _):
        d_ref[pl.ds(n * 4, 4), :] = hs_ref[pl.ds(away_ref[n] * 4, 4), :]
        return 0

    lax.fori_loop(0, 128, one, 0, unroll=8)
    lax.fori_loop(0, 32 * SLOTS, away, 0, unroll=8)


def make_slice(slice_list, away_list, hs, recv):
    return pl.pallas_call(
        slice_kernel,
        out_shape=[
            jax.ShapeDtypeStruct((512, LANES), F32),
            jax.ShapeDtypeStruct((32 * SLOTS * 4, LANES), F32),
        ],
        in_specs=[pl.BlockSpec(memory_space=pltpu.SMEM)] * 2 + [pl.BlockSpec(memory_space=pltpu.VMEM)] * 2,
        out_specs=[pl.BlockSpec(memory_space=pltpu.VMEM)] * 2,
        compiler_params=pltpu.CompilerParams(vmem_limit_bytes=16 << 20),
        name="pivot_slice",
    )(slice_list, away_list, hs, recv)


def patch_kernel(row_ref, y_ref, x_ref, recv_ref, o_ref, p_ref):
    o_ref[...] = x_ref[...]

    def one(n, _):
        row, y = row_ref[n], y_ref[n]
        h, s = n // CAP, (n % CAP) // 4

        @pl.when(row >= 0)
        def _():
            for k in range(4):
                piece = recv_ref[pl.ds(((y * 8 + 2 * k + h) * SLOTS + s) * 4, 4), :]
                o_ref[pl.ds(row * SUB + k, 4, stride=4), :] = piece

        return 0

    lax.fori_loop(0, 2 * CAP, one, 0)
    for j in range(4):
        p_ref[:, j * 128 : (j + 1) * 128] = o_ref[pl.ds(j, NB, stride=SUB), :]


def patch(to_row, from_y, x, recv):
    return pl.pallas_call(
        patch_kernel,
        out_shape=[
            jax.ShapeDtypeStruct((NB * SUB, LANES), F32),
            jax.ShapeDtypeStruct((NB, NB), F32),
        ],
        in_specs=[pl.BlockSpec(memory_space=pltpu.SMEM)] * 2 + [pl.BlockSpec(memory_space=pltpu.VMEM)] * 2,
        out_specs=[pl.BlockSpec(memory_space=pltpu.VMEM)] * 2,
        compiler_params=pltpu.CompilerParams(vmem_limit_bytes=24 << 20),
        name="patch_rows",
    )(to_row, from_y, x, recv)


OFF_Y = (0, -1, 1, 2)
OFF_Z = (0, -1, 1, -2, 2, -3, 3, 4)


def update_kernel(info_ref, x_ref, m0_ref, l1_ref, sp_ref, *refs):
    parts, (o_ref, uh, ul, mh, ml) = refs[:-5], refs[-5:]
    y, z, home, special = info_ref[0], info_ref[1], info_ref[2], info_ref[3]

    def stage(v, dy, dz, q):
        yy = lax.rem(y + (dy + 4), 4)
        zz = lax.rem(z + (dz + 8), 8)
        row = pl.multiple_of(lax.rem(zz, 2) * 512 + yy * 128, 128)
        col = pl.multiple_of((4 * q + zz // 2) * 128, 128)
        hi = v.astype(jnp.bfloat16)
        uh[pl.ds(row, 128), pl.ds(col, 128)] = hi
        ul[pl.ds(row, 128), pl.ds(col, 128)] = (v - hi.astype(F32)).astype(jnp.bfloat16)

    for a, m_ref in ((0, m0_ref), (1, l1_ref)):
        m = m_ref[...]
        hi = m.astype(jnp.bfloat16)
        mh[:, a * 512 : (a + 1) * 512] = hi
        ml[:, a * 512 : (a + 1) * 512] = (m - hi.astype(F32)).astype(jnp.bfloat16)
    a_parts, b_parts = parts[:9], parts[9:]
    for n, dz in enumerate(OFF_Z[:7]):
        for m, dy in enumerate(OFF_Y):
            for q in range(2):
                stage(a_parts[n][m, q], dy, dz, q)
    for half in range(2):
        for m in range(2):
            for q in range(2):
                stage(a_parts[7 + half][m, q], OFF_Y[2 * half + m], 4, q)
    for n, dy in enumerate(OFF_Y[:3]):
        for m, dz in enumerate(OFF_Z):
            for q in range(2):
                stage(b_parts[n][m, q], dy, dz, 2 + q)
    for half in range(2):
        for m in range(4):
            for q in range(2):
                stage(b_parts[3 + half][m, q], 2, OFF_Z[4 * half + m], 2 + q)

    for n in range(8):
        cols = slice(n * 256, (n + 1) * 256)
        dot = functools.partial(jnp.dot, preferred_element_type=F32)
        acc = dot(mh[...], uh[:, cols]) + dot(mh[...], ul[:, cols]) + dot(ml[...], uh[:, cols])
        for s in range(2):
            j = 2 * n + s
            base = x_ref[pl.ds(j, NB, stride=SUB), :]
            new = jnp.where(home > 0, 0.0, base) - acc[:, s * 128 : (s + 1) * 128]
            if n < 2:
                new = jnp.where(special > 0, sp_ref[:, j * 128 : (j + 1) * 128], new)
            o_ref[pl.ds(j, NB, stride=SUB), :] = new


def update(info, x, m0, l1, special, parts):
    n = 4 + len(parts)
    return pl.pallas_call(
        update_kernel,
        out_shape=jax.ShapeDtypeStruct((NB * SUB, LANES), F32),
        in_specs=[pl.BlockSpec(memory_space=pltpu.SMEM)] + [pl.BlockSpec(memory_space=pltpu.VMEM)] * n,
        out_specs=pl.BlockSpec(memory_space=pltpu.VMEM),
        scratch_shapes=[
            pltpu.VMEM((1024, 2048), jnp.bfloat16),
            pltpu.VMEM((1024, 2048), jnp.bfloat16),
            pltpu.VMEM((512, 1024), jnp.bfloat16),
            pltpu.VMEM((512, 1024), jnp.bfloat16),
        ],
        compiler_params=pltpu.CompilerParams(vmem_limit_bytes=48 << 20),
        name="update",
    )(info, x, m0, l1, special, *parts)


def shift(v, axis, step):
    n = {"y": Y, "z": Z, "x": X, "core": CORE}[axis]
    return lax.ppermute(v, axis, [(i, (i + step) % n) for i in range(n)])


def scatter_home(blocks, y, z):
    go = lambda v, a, b: lax.ppermute(v, ROW, [(a * Z + h, b * Z + h) for h in range(2)])
    far_a = go(blocks[2, :2], 0, 1)
    far_b = go(blocks[2, 2:], 0, 3)
    near_a = go(blocks[1], 0, 1)
    near_b = go(blocks[3], 0, 3)
    far = jnp.concatenate([go(far_a, 1, 2), go(far_b, 3, 2)])
    block = jnp.where(y == 0, blocks[0], near_a + near_b + far)
    out = jnp.where(z < 2, block[0], 0.0)
    for k in range(1, 4):
        pairs = [(i * Z + h, i * Z + 2 * k + h) for i in range(Y) for h in range(2)]
        out = out + lax.ppermute(block[k], ROW, pairs)
    return out


def gather_y_then_z(s):
    up, down = shift(s, "y", 1), shift(s, "y", -1)
    block = jnp.stack([s, up, down, shift(up, "y", 1)])
    parts, up, down = [block], block, block
    for _ in range(3):
        up, down = shift(up, "z", 1), shift(down, "z", -1)
        parts += [up, down]
    return parts + [shift(up[:2], "z", 1), shift(down[2:], "z", -1)]


def gather_z_then_y(s):
    parts, up, down = [s], s, s
    for _ in range(3):
        up, down = shift(up, "z", 1), shift(down, "z", -1)
        parts += [up, down]
    block = jnp.stack(parts + [shift(up, "z", 1)])
    up, down = shift(block, "y", 1), shift(block, "y", -1)
    return [block, up, down, shift(up[:4], "y", 1), shift(down[4:], "y", -1)]


def spread_x(v, x):
    go = lambda u, a, b: lax.ppermute(u, "x", [(a, b)])
    half = v.shape[0] // 2
    one, three = go(v, 0, 1), go(v, 0, 3)
    two = jnp.concatenate([go(one[:half], 1, 2), go(three[half:], 3, 2)])
    return jnp.where(x == 0, v, one + three + two)


def body(matrix, pivots, inverses):
    y, z = lax.axis_index("y"), lax.axis_index("z")
    x, core = lax.axis_index("x"), lax.axis_index("core")
    r = y * Z + z
    c = x * CORE + core
    work = matrix.reshape(NB * SUB, LANES)
    home_list, give_list, slice_list, away_list, to_row, from_y, hot, over = plan(pivots, y, z)

    with jax.named_scope("rows_out"):
        blocks, send = pack(home_list, give_list, work)
        recv = lax.all_to_all(send.reshape(32, 4 * SLOTS, LANES), ROW, 0, 0)
        hs = scatter_home(blocks.reshape(4, 4, 512, LANES), y, z)
    with jax.named_scope("pivot_slice"):
        mine, away = make_slice(slice_list, away_list, hs, recv.reshape(-1, LANES))
        mine = mine.reshape(4, 128, LANES)
    with jax.named_scope("gather_rows"):
        parts = gather_y_then_z(mine[:2]) + gather_z_then_y(mine[2:])
    with jax.named_scope("panel_pieces"):
        piece = mine[0]
        other = shift(piece, "core", 1)
        piece = jnp.where(core == 1 - z % 2, piece, other)
        half = lax.dynamic_slice_in_dim(piece, core * 64, 64, 0)
        half = spread_x(half, x)
        ours = lax.all_gather(half, ROW, axis=0)
        theirs = shift(ours, "core", 1)
        both = jnp.stack([jnp.where(core == 0, ours, theirs), jnp.where(core == 0, theirs, ours)])
        both = both.reshape(2, Y, 4, 2, 64, LANES).transpose(3, 1, 0, 4, 2, 5).reshape(2, NB, NB)
        u01, p0 = both[0], both[1]
    with jax.named_scope("rows_in"):
        recv = lax.all_to_all(away.reshape(32, 4 * SLOTS, LANES), ROW, 0, 0)
        work2, panel = patch(to_row, from_y, work, recv.reshape(-1, LANES))
    with jax.named_scope("panel_columns"):
        panel = spread_x(panel, x)
        swapped = shift(panel, "core", 1)
        a0 = jnp.where(core == 0, panel, swapped)
        a1 = jnp.where(core == 0, swapped, panel)
    with jax.named_scope("factors"):
        dot = functools.partial(jnp.dot, precision=HIGHEST)
        inv0, inv1 = inverses[0], inverses[1]
        inv0p, inv1p = dot(inv0, hot[0]), dot(inv1, hot[1])
        a0 = jnp.where(r == 1, dot(hot[1], p0), a0)
        l0 = dot(a0, inv0p)
        rest = a1 - dot(l0, u01)
        l1 = dot(rest, inv1p)
        lp0 = dot(p0, inv0p)
        m0 = jnp.where(r == 0, -hot[0], jnp.where(r == 1, l0, l0 - dot(l1, lp0)))
        l1 = jnp.where(r == 0, 0.0, jnp.where(r == 1, -hot[1], l1))
        special = dot(jnp.where(c == 0, a0, rest), jnp.where(c == 0, inv0, inv1))
    with jax.named_scope("update"):
        is_special = ((c == 0) & (r >= 1)) | ((c == 1) & (r >= 2))
        info = jnp.stack([y, z, (r < 2).astype(I32), is_special.astype(I32)])
        out = update(info, work2, m0, l1, special, parts)
    out = lax.cond(over, lambda o: general(work, pivots, inverses), lambda o: o, out)
    return out.reshape(matrix.shape)


def solution(mesh):
    grid = Mesh(mesh.devices.reshape(Y, Z, X, CORE), ("y", "z", "x", "core"))
    placed = (P(None, ROW, None, None, COL, None), P(), P())
    return jax.shard_map(
        body,
        mesh=grid,
        in_specs=placed,
        out_specs=P(None, ROW, None, None, COL, None),
        check_vma=False,
    )
```

```python
import functools

import jax
import jax.numpy as jnp
from jax import lax
from jax.experimental import pallas as pl
from jax.experimental.pallas import tpu as pltpu
from jax.sharding import Mesh, PartitionSpec as P

Y, Z, X, CORE = 4, 8, 4, 2
NB = 512
LANES = 128
SUB = 16
SLOTS = 8
CAP = 4 * SLOTS
KEEP = 32
REST = 128 - KEEP
WAVE = 4 * KEEP + REST
ROW = ("y", "z")
COL = ("x", "core")
HIGHEST = lax.Precision.HIGHEST
F32 = jnp.float32
I32 = jnp.int32


def from_root(x, axis, root):
    mine = lax.axis_index(axis) == root
    return lax.psum(jnp.where(mine, x, jnp.zeros_like(x)), axis)


def general(work, pivots, inverses):
    row_index = lax.axis_index(ROW)
    col_index = lax.axis_index(COL)
    work = work.reshape(NB, SUB * LANES)
    row_ids = row_index * NB + jnp.arange(NB, dtype=I32)
    col_ids = (
        (jnp.arange(4, dtype=I32)[:, None] * 8 + col_index) * NB
        + jnp.arange(NB, dtype=I32)[None, :]
    ).reshape(-1)
    for panel in range(2):
        after_row = (panel + 1) * NB
        targets = pivots[panel]
        held = targets // NB == row_index
        local_row = targets % NB
        picked = jnp.where(held[:, None], jnp.take(work, local_row, axis=0), 0.0)
        u_rows = lax.psum(picked, ROW)
        displaced = from_root(work, ROW, panel)
        dest_row = jnp.where(held, local_row, NB)
        work = work.at[dest_row].set(displaced, mode="drop")
        work = jnp.where(row_index == panel, u_rows, work)
        panel_cols = work[:, :NB]
        product = jnp.dot(panel_cols, inverses[panel], precision=HIGHEST)
        l_cols = from_root(product, COL, panel)
        below_mask = (row_ids >= after_row)[:, None]
        work = work.at[:, :NB].set(
            jnp.where(below_mask & (col_index == panel), l_cols, panel_cols)
        )
        update = jnp.dot(l_cols, u_rows, precision=HIGHEST)
        trail_mask = below_mask & (col_ids >= after_row)[None, :]
        work = jnp.where(trail_mask, work - update, work)
    return work.reshape(NB * SUB, LANES)


def ranks(key):
    t = jnp.arange(NB, dtype=I32)
    same = (key[:, None] == key[None, :]) & (t[None, :] < t[:, None])
    less = key[None, :] < key[:, None]
    rank = jnp.sum(same.astype(I32), axis=1)
    place = rank + jnp.sum(less.astype(I32), axis=1)
    return rank, place


def plan(pivots, y, z):
    r = y * Z + z
    t = jnp.arange(NB, dtype=I32)
    piv0, piv1 = pivots[0], pivots[1]
    meet = piv1[:, None] == piv0[None, :]
    src1 = jnp.where(jnp.any(meet, 1), jnp.sum(jnp.where(meet, t[None, :], 0), 1), piv1)
    src = (piv0, src1)
    in_home = piv0[:, None] == NB + t[None, :]
    moved = piv0[:, None] == piv1[None, :]
    dst0 = jnp.where(
        jnp.any(in_home, 1),
        jnp.sum(jnp.where(in_home, piv1[None, :], 0), 1),
        jnp.where(jnp.any(moved, 1), NB + jnp.sum(jnp.where(moved, t[None, :], 0), 1), piv0),
    )
    taken = (NB + t)[:, None] == piv0[None, :]
    dst1 = jnp.where(jnp.any(taken, 1), jnp.sum(jnp.where(taken, t[None, :], 0), 1), piv1)
    dst = (dst0, dst1)

    k_rank, k_place, k_key = [], [], []
    h_rank, h_place, h_key = [], [], []
    for h in range(2):
        own = h * NB + t
        stay = src[h] == own
        key = jnp.where(stay, -1, src[h] // NB)
        rank, place = ranks(key)
        k_key.append(key), k_rank.append(rank), k_place.append(place)
        away = dst[h] >= 2 * NB
        hkey = jnp.where(stay, -1, jnp.where(away, dst[h] // NB, 32))
        rank, place = ranks(hkey)
        h_key.append(hkey), h_rank.append(rank), h_place.append(place)
    over = jnp.zeros((), jnp.bool_)
    for h in range(2):
        over = over | jnp.any((k_key[h] >= 0) & (k_rank[h] >= CAP))
        over = over | jnp.any((h_key[h] >= 0) & (h_key[h] < 32) & (h_rank[h] >= CAP))
        over = over | jnp.any((h_key[h] < 0) & (h_rank[h] >= 4 * KEEP))

    def spot(place):
        return (place % 4) * 128 + place // 4

    mine = z % 2
    pick = lambda pair: jnp.where(mine == 0, pair[0], pair[1])
    home_spot = spot(pick(h_place))
    home_list = jnp.sum(jnp.where(home_spot[None, :] == t[:, None], t[None, :], 0), 1)
    e = jnp.arange(4 * SLOTS, dtype=I32)
    give = []
    for h in range(2):
        code = jnp.where(k_key[h] == r, (k_place[h] % 4) * SLOTS + k_rank[h] // 4, -1)
        code = jnp.where(k_rank[h] < CAP, code, -1)
        give.append(jnp.sum(jnp.where(code[None, :] == e[:, None], (src[h] % NB)[None, :], 0), 1))
    give_list = jnp.concatenate(give)
    place, key, rank = pick(k_place), pick(k_key), pick(k_rank)
    code = jnp.where(key < 0, -1, jnp.minimum(key * SLOTS + rank // 4, 32 * SLOTS - 1))
    i = jnp.arange(128, dtype=I32) * 4 + y
    slice_list = jnp.sum(jnp.where(place[None, :] == i[:, None], code[None, :], 0), 1)
    place, key, rank = pick(h_place), pick(h_key), pick(h_rank)
    ok = (place % 4 == y) & (key >= 0) & (key < 32) & (rank < CAP)
    code = jnp.where(ok, key * SLOTS + rank // 4, -1)
    e = jnp.arange(32 * SLOTS, dtype=I32)
    away_list = jnp.sum(jnp.where(code[None, :] == e[:, None], (place // 4)[None, :], 0), 1)
    e = jnp.arange(CAP, dtype=I32)
    to_row, from_y = [], []
    for h in range(2):
        hit = ((h_key[h] == r)[None, :]) & (h_rank[h][None, :] == e[:, None])
        to_row.append(jnp.sum(jnp.where(hit, (dst[h] % NB + 1)[None, :], 0), 1) - 1)
        from_y.append(jnp.sum(jnp.where(hit, (h_place[h] % 4)[None, :], 0), 1))
    to_row, from_y = jnp.concatenate(to_row), jnp.concatenate(from_y)
    hot = [jnp.broadcast_to(spot(k_place[h])[:, None], (NB, LANES)) for h in range(2)]
    return home_list, give_list, slice_list, away_list, to_row, from_y, hot, over


VMEM = pl.BlockSpec(memory_space=pltpu.VMEM)
SMEM = pl.BlockSpec(memory_space=pltpu.SMEM)


def call(kernel, name, out_shape, in_specs, mib, us, scratch=(), alias=None, out_specs=None):
    return pl.pallas_call(
        kernel,
        out_shape=out_shape,
        in_specs=in_specs,
        out_specs=[VMEM] * len(out_shape) if out_specs is None else out_specs,
        scratch_shapes=list(scratch),
        input_output_aliases=alias or {},
        compiler_params=pltpu.CompilerParams(vmem_limit_bytes=mib << 20),
        cost_estimate=pl.CostEstimate(flops=0, bytes_accessed=us * 3_000_000, transcendentals=0),
        name=name,
    )


def shaped(*shape, dtype=F32):
    return jax.ShapeDtypeStruct(shape, dtype)


def pack_kernel(home_ref, give_ref, x_ref, h_ref, rest_ref, g_ref):
    def give(n, _):
        row = give_ref[n] * SUB
        h, y, s = n // (4 * SLOTS), (n // SLOTS) % 4, n % SLOTS
        for k in range(4):
            g_ref[pl.ds(((y * 8 + 2 * k + h) * SLOTS + s) * 4, 4), :] = x_ref[pl.ds(row + k, 4, stride=4), :]
        return 0

    def keep(n, _):
        y, i = n // KEEP, n % KEEP
        row = home_ref[y * 128 + i] * SUB
        for k in range(4):
            h_ref[pl.ds((y * 4 + k) * WAVE + i * 4, 4), :] = x_ref[pl.ds(row + k, 4, stride=4), :]
        return 0

    def rest(n, _):
        y, i = n // REST, n % REST
        row = home_ref[y * 128 + KEEP + i] * SUB
        for k in range(4):
            h_ref[pl.ds((y * 4 + k) * WAVE + 4 * KEEP + i, 1), :] = x_ref[pl.ds(row + k, 1), :]
            rest_ref[pl.ds(((y * 4 + k) * REST + i) * 3, 3), :] = x_ref[pl.ds(row + 4 + k, 3, stride=4), :]
        return 0

    lax.fori_loop(0, 8 * SLOTS, give, 0, unroll=8)
    lax.fori_loop(0, 4 * KEEP, keep, 0, unroll=8)
    lax.fori_loop(0, 4 * REST, rest, 0, unroll=8)


def pack(home_list, give_list, x):
    out = [shaped(16 * WAVE, LANES), shaped(16 * REST * 3, LANES), shaped(32 * SLOTS * 4, LANES)]
    return call(pack_kernel, "pack", out, [SMEM, SMEM, VMEM], 24, 8)(home_list, give_list, x)


def slice_kernel(slice_ref, hs_ref, recv_ref, s_ref):
    def one(i, _):
        code = slice_ref[i]
        theirs = recv_ref[pl.ds(jnp.maximum(code, 0) * 4, 4), :]
        here = hs_ref[pl.ds(jnp.minimum(i, KEEP - 1) * 4, 4), :]
        s_ref[pl.ds(i, 4, stride=128), :] = jnp.where(code < 0, here, theirs)
        return 0

    lax.fori_loop(0, 128, one, 0, unroll=8)


def make_slice(slice_list, hs, recv):
    return call(slice_kernel, "pivot_slice", [shaped(512, LANES)], [SMEM, VMEM, VMEM], 16, 2)(slice_list, hs, recv)[0]


def away_kernel(away_ref, keep_ref, d_ref):
    def away(n, _):
        i = away_ref[n]
        d_ref[pl.ds(n, 1), :] = keep_ref[pl.ds(jnp.where(i < KEEP, i * 4, i + 3 * KEEP), 1), :]
        return 0

    lax.fori_loop(0, 32 * SLOTS, away, 0, unroll=8)


def make_away(away_list, keep):
    out = [shaped(32 * SLOTS, LANES)]
    return call(away_kernel, "away_first", out, [SMEM, VMEM], 16, 1)(away_list, keep)[0]


def away_rest_kernel(away_ref, keep_ref, rest_ref, d_ref):
    def away(n, _):
        i = away_ref[n]
        a = keep_ref[pl.ds(jnp.minimum(i, KEEP - 1) * 4 + 1, 3), :]
        b = rest_ref[pl.ds(jnp.maximum(i - KEEP, 0) * 3, 3), :]
        d_ref[pl.ds(n * 3, 3), :] = jnp.where(i < KEEP, a, b)
        return 0

    lax.fori_loop(0, 32 * SLOTS, away, 0, unroll=8)


def make_away_rest(away_list, keep, rest):
    out = [shaped(32 * SLOTS * 3, LANES)]
    return call(away_rest_kernel, "away_rest", out, [SMEM, VMEM, VMEM], 16, 2)(away_list, keep, rest)[0]


def patch_kernel(row_ref, y_ref, x_ref, first_ref, rest_ref, o_ref):
    o_ref[...] = x_ref[...]

    def one(n, _):
        row, y = row_ref[n], y_ref[n]
        h, s = n // CAP, (n % CAP) // 4

        @pl.when(row >= 0)
        def _():
            o_ref[pl.ds(row * SUB, 4), :] = first_ref[pl.ds((y * 8 + h) * SLOTS + s, 4, stride=2 * SLOTS), :]
            for k in range(4):
                piece = rest_ref[pl.ds(((y * 8 + 2 * k + h) * SLOTS + s) * 3, 3), :]
                o_ref[pl.ds(row * SUB + 4 + k, 3, stride=4), :] = piece

        return 0

    lax.fori_loop(0, 2 * CAP, one, 0)


def patch(to_row, from_y, x, first, rest):
    out = [shaped(NB * SUB, LANES)]
    return call(patch_kernel, "patch_rows", out, [SMEM] * 2 + [VMEM] * 3, 24, 4)(to_row, from_y, x, first, rest)[0]


def split(v):
    hi = v.astype(jnp.bfloat16)
    return hi, (v - hi.astype(F32)).astype(jnp.bfloat16)


def dot3(a, b):
    dot = functools.partial(jnp.dot, preferred_element_type=F32)
    return dot(a[0], b[0]) + dot(a[0], b[1]) + dot(a[1], b[0])


OFF_X = (0, -1, 1, 2)


def factor_kernel(
    info_ref, row_ref, y_ref, own_ref, swap_ref, late_ref, late_swap, piece_ref, piece_swap,
    inv0_ref, inv1_ref, spot0_ref, spot1_ref,
    m_ref, sp_ref, a0, a1, u01, p0, lin0, lin1,
):
    r, c, x, core = info_ref[4], info_ref[5], info_ref[6], info_ref[7]
    first = core == 0
    own, other = own_ref[...], swap_ref[...]
    lin0[...] = jnp.where(first, own, other)
    lin1[...] = jnp.where(first, other, own)

    def one(n, _):
        row, y = row_ref[n], y_ref[n]
        h, s = n // CAP, (n % CAP) // 4

        @pl.when(row >= 0)
        def _():
            at = pl.ds((y * 8 + h) * SLOTS + s, 4, stride=2 * SLOTS)
            own, other = late_ref[at, :], late_swap[at, :]
            lin0[pl.ds(row * 4, 4), :] = jnp.where(first, own, other)
            lin1[pl.ds(row * 4, 4), :] = jnp.where(first, other, own)

        return 0

    lax.fori_loop(0, 2 * CAP, one, 0)
    for j in range(4):
        cols = slice(j * 128, (j + 1) * 128)
        a0[:, cols] = lin0[pl.ds(j, NB, stride=4), :]
        a1[:, cols] = lin1[pl.ds(j, NB, stride=4), :]
    for m, dx in enumerate(OFF_X):
        for ref, cc in ((piece_ref, core), (piece_swap, 1 - core)):
            part = lax.rem(x + (dx + 4), 4) * 2 + cc
            for yy in range(4):
                rows = pl.ds(pl.multiple_of(yy * 128 + part * 16, 16), 16)
                for k in range(4):
                    cols = slice(k * 128, (k + 1) * 128)
                    u01[rows, cols] = ref[m, yy * 8 + 2 * k]
                    p0[rows, cols] = ref[m, yy * 8 + 2 * k + 1]

    dot = functools.partial(jnp.dot, preferred_element_type=F32)
    place = lax.broadcasted_iota(I32, (NB, NB), 1)
    hot0 = jnp.where(spot0_ref[:, :1] == place, 1.0, 0.0)
    hot1 = jnp.where(spot1_ref[:, :1] == place, 1.0, 0.0)
    inv0, inv1 = split(inv0_ref[...]), split(inv1_ref[...])

    def turned(inv, hot):
        hot = hot.astype(jnp.bfloat16)
        return tuple(dot(v, hot).astype(jnp.bfloat16) for v in inv)

    inv0p, inv1p = turned(inv0, hot0), turned(inv1, hot1)
    p0s = split(p0[...])

    @pl.when(r == 1)
    def _():
        at = hot1.astype(jnp.bfloat16)
        a0[...] = dot(at, p0s[0]) + dot(at, p0s[1])

    def put(at, v):
        hi, lo = split(v)
        m_ref[:NB, at : at + NB] = hi
        m_ref[NB:, at : at + NB] = lo

    l0 = dot3(split(a0[...]), inv0p)
    a1[...] = a1[...] - dot3(split(l0), split(u01[...]))
    l1 = dot3(split(a1[...]), inv1p)
    lp0 = dot3(p0s, inv0p)
    m0 = jnp.where(r == 1, l0, l0 - dot3(split(l1), split(lp0)))
    put(0, jnp.where(r == 0, -hot0, m0))
    put(NB, jnp.where(r == 0, 0.0, jnp.where(r == 1, -hot1, l1)))

    @pl.when(c == 0)
    def _():
        sp_ref[...] = dot3(split(a0[...]), inv0)

    @pl.when(c != 0)
    def _():
        sp_ref[...] = dot3(split(a1[...]), inv1)


def factors(info, to_row, from_y, *rest):
    out = [shaped(2 * NB, 2 * NB, dtype=jnp.bfloat16), shaped(NB, NB)]
    scratch = [pltpu.VMEM((NB, NB), F32)] * 4 + [pltpu.VMEM((NB * 4, LANES), F32)] * 2
    specs = [SMEM] * 3 + [VMEM] * len(rest)
    return call(factor_kernel, "factors", out, specs, 48, 12, scratch)(info, to_row, from_y, *rest)


OFF_Y = (0, -1, 1, 2)


def update_kernel(info_ref, x_ref, m_ref, sp_ref, u_ref, o_ref, uh, ul):
    i = pl.program_id(0)
    y, home, special = info_ref[0], info_ref[2], info_ref[3]
    x2, o2 = x_ref.reshape(NB * 8, LANES), o_ref.reshape(NB * 8, LANES)
    for m, dy in enumerate(OFF_Y):
        at = lax.rem(y + (dy + 4), 4) * 128
        for zz in range(4):
            rows = pl.ds(pl.multiple_of((zz % 2) * 512 + at, 128), 128)
            cols = slice(zz // 2 * 128, zz // 2 * 128 + 128)
            uh[rows, cols], ul[rows, cols] = split(u_ref[zz, m, 0])
    dot = functools.partial(jnp.dot, preferred_element_type=F32)
    both = dot(m_ref[...], uh[...])
    acc = both[:NB] + both[NB:] + dot(m_ref[:NB, :], ul[...])
    for s in range(2):
        j = 2 * lax.rem(i, 4) + s
        base = x2[pl.ds(j, NB, stride=8), :]
        new = jnp.where(home > 0, 0.0, base) - acc[:, s * 128 : (s + 1) * 128]
        put = sp_ref[:, pl.ds(pl.multiple_of(lax.rem(j, 4) * 128, 128), 128)]
        o2[pl.ds(j, NB, stride=8), :] = jnp.where((special > 0) & (i < 2), put, new)


def update(info, x, m, special, rows):
    half = pl.BlockSpec((NB, 8, LANES), lambda i: (0, i // 4, 0))
    whole = pl.BlockSpec((2 * NB, 2 * NB), lambda i: (0, 0))
    tile = pl.BlockSpec((4, 4, 1, 128, 128), lambda i: (i % 2, 0, i // 2, 0, 0))
    return pl.pallas_call(
        update_kernel,
        out_shape=shaped(NB, SUB, LANES),
        grid=(8,),
        in_specs=[SMEM, half, whole, pl.BlockSpec((NB, NB), lambda i: (0, 0)), tile],
        out_specs=half,
        scratch_shapes=[pltpu.VMEM((1024, 256), jnp.bfloat16)] * 2,
        compiler_params=pltpu.CompilerParams(vmem_limit_bytes=60 << 20),
        cost_estimate=pl.CostEstimate(flops=0, bytes_accessed=30_000_000, transcendentals=0),
        name="update",
    )(info, x, m, special, rows)


def join_kernel(count, *refs):
    parts, outs = refs[:-count], refs[-count:]
    each = len(parts) // count
    for n, ref in enumerate(parts):
        outs[n // each][n % each] = ref[...]


def join(parts, count=1):
    out = [shaped(len(parts) // count, *parts[0].shape)] * count
    return call(functools.partial(join_kernel, count), "join", out, [VMEM] * len(parts), 16, 1)(*parts)


def shift(v, axis, step):
    n = {"y": Y, "z": Z, "x": X, "core": CORE}[axis]
    return lax.ppermute(v, axis, [(i, (i + step) % n) for i in range(n)])


def tie(*values):
    return lax.optimization_barrier(values)


def scatter_y(blocks):
    go = lambda b: lax.ppermute(blocks[b], ROW, [(h, b * Z + h) for h in range(2)])
    return go(2), go(1), go(3)


def scatter_z(block):
    out = []
    for k in (2, 1, 3):
        pairs = [(i * Z + h, i * Z + 2 * k + h) for i in range(Y) for h in range(2)]
        out.append(lax.ppermute(block[k], ROW, pairs))
    return out


def body(matrix, pivots, inverses):
    y, z = lax.axis_index("y"), lax.axis_index("z")
    x, core = lax.axis_index("x"), lax.axis_index("core")
    r = y * Z + z
    c = x * CORE + core
    work = matrix.reshape(NB * SUB, LANES)
    panel = work.reshape(NB, SUB, LANES)[:, :4].reshape(NB * 4, LANES)
    panel = jnp.where(x == 0, panel, 0.0)
    home_list, give_list, slice_list, away_list, to_row, from_y, hot, over = plan(pivots, y, z)
    is_special = ((c == 0) & (r >= 1)) | ((c == 1) & (r >= 2))
    info = jnp.stack([y, z, (r < 2).astype(I32), is_special.astype(I32), r, c, x, core])
    inv0, inv1 = inverses[0], inverses[1]

    keep, rest, send = pack(home_list, give_list, work)
    keep, rest = keep.reshape(4, 4, WAVE, LANES), rest.reshape(4, 4, REST * 3, LANES)
    keep_y = scatter_y(keep)
    recv = lax.all_to_all(send.reshape(32, 4 * SLOTS, LANES), ROW, 0, 0)
    keep = jnp.where(y == 0, keep[0], sum(keep_y))
    keep_z = scatter_z(keep)
    keep, panel, to_row, from_y, spot0, spot1, *keep_z = tie(keep, panel, to_row, from_y, *hot, *keep_z)
    keep = jnp.where(z < 2, keep[0], sum(keep_z))
    panel = lax.psum(panel, "x")
    mine = make_slice(slice_list, keep, recv.reshape(-1, LANES)).reshape(4, 128, LANES)

    parts = [shift(mine, "y", n) for n in (1, -1, 2)]
    away = make_away(away_list, keep)
    away, rest, *parts = tie(away, rest, *parts)
    rows = lax.all_gather(join([mine] + parts)[0], "z", axis=0)

    recv_first = lax.all_to_all(away.reshape(32, SLOTS, LANES), ROW, 0, 0)
    rest_y = scatter_y(rest)
    piece = lax.all_to_all(mine[0].reshape(8, 16, LANES), COL, 0, 0)
    piece, recv_first, *rest_y = tie(piece, recv_first, *rest_y)
    rest = jnp.where(y == 0, rest[0], sum(rest_y))
    rest_z = scatter_z(rest)
    piece = lax.dynamic_slice_in_dim(piece, 1 - z % 2, 1, 0)
    piece = lax.all_to_all(jnp.broadcast_to(piece, (32, 16, LANES)), ROW, 0, 0)
    late = recv_first.reshape(-1, LANES)
    late_x = [lax.ppermute(late, "x", [(0, b)]) for b in (2, 1, 3)]
    piece, la, lb, lc, *rest_z = tie(piece, *late_x, *rest_z)
    late = jnp.where(x == 0, late, la + lb + lc)
    late_swap = shift(late, "core", 1)
    pieces = [shift(piece, "x", n) for n in (1, -1, 2)]
    swap = shift(panel, "core", 1)
    rest = jnp.where(z < 2, rest[0], sum(rest_z))
    away = make_away_rest(away_list, keep, rest)
    recv_rest = lax.all_to_all(away.reshape(32, SLOTS * 3, LANES), ROW, 0, 0)
    recv_rest, late_swap, swap, *pieces = tie(recv_rest, late_swap, swap, *pieces)
    piece = join([piece] + pieces)[0]
    piece_swap = shift(piece, "core", 1)
    base = patch(to_row, from_y, work, recv_first.reshape(-1, LANES), recv_rest.reshape(-1, LANES))
    m, special = factors(
        info, to_row, from_y, panel, swap, late, late_swap, piece, piece_swap, inv0, inv1, spot0, spot1,
    )
    out = update(info, base.reshape(NB, SUB, LANES), m, special, rows)
    out = out.reshape(NB * SUB, LANES)
    out = lax.cond(over, lambda o: general(work, pivots, inverses), lambda o: o, out)
    return out.reshape(matrix.shape)


def solution(mesh):
    grid = Mesh(mesh.devices.reshape(Y, Z, X, CORE), ("y", "z", "x", "core"))
    placed = (P(None, ROW, None, None, COL, None), P(), P())
    return jax.shard_map(
        body,
        mesh=grid,
        in_specs=placed,
        out_specs=P(None, ROW, None, None, COL, None),
        check_vma=False,
    )
```

```python
import functools

import jax
import jax.numpy as jnp
from jax import lax
from jax.experimental import pallas as pl
from jax.experimental.pallas import tpu as pltpu
from jax.sharding import Mesh, PartitionSpec as P

Y, Z, X, CORE = 4, 8, 4, 2
NB = 512
LANES = 128
SUB = 16
SLOTS = 8
CAP = 4 * SLOTS
KEEP = 32
REST = 128 - KEEP
WAVE = 4 * KEEP + REST
ROW = ("y", "z")
COL = ("x", "core")
HIGHEST = lax.Precision.HIGHEST
F32 = jnp.float32
I32 = jnp.int32


def from_root(x, axis, root):
    mine = lax.axis_index(axis) == root
    return lax.psum(jnp.where(mine, x, jnp.zeros_like(x)), axis)


def general(work, pivots, inverses):
    row_index = lax.axis_index(ROW)
    col_index = lax.axis_index(COL)
    work = work.reshape(NB, SUB * LANES)
    row_ids = row_index * NB + jnp.arange(NB, dtype=I32)
    col_ids = (
        (jnp.arange(4, dtype=I32)[:, None] * 8 + col_index) * NB
        + jnp.arange(NB, dtype=I32)[None, :]
    ).reshape(-1)
    for panel in range(2):
        after_row = (panel + 1) * NB
        targets = pivots[panel]
        held = targets // NB == row_index
        local_row = targets % NB
        picked = jnp.where(held[:, None], jnp.take(work, local_row, axis=0), 0.0)
        u_rows = lax.psum(picked, ROW)
        displaced = from_root(work, ROW, panel)
        dest_row = jnp.where(held, local_row, NB)
        work = work.at[dest_row].set(displaced, mode="drop")
        work = jnp.where(row_index == panel, u_rows, work)
        panel_cols = work[:, :NB]
        product = jnp.dot(panel_cols, inverses[panel], precision=HIGHEST)
        l_cols = from_root(product, COL, panel)
        below_mask = (row_ids >= after_row)[:, None]
        work = work.at[:, :NB].set(
            jnp.where(below_mask & (col_index == panel), l_cols, panel_cols)
        )
        update = jnp.dot(l_cols, u_rows, precision=HIGHEST)
        trail_mask = below_mask & (col_ids >= after_row)[None, :]
        work = jnp.where(trail_mask, work - update, work)
    return work.reshape(NB * SUB, LANES)


def ranks(key):
    t = jnp.arange(NB, dtype=I32)
    same = (key[:, None] == key[None, :]) & (t[None, :] < t[:, None])
    less = key[None, :] < key[:, None]
    rank = jnp.sum(same.astype(I32), axis=1)
    place = rank + jnp.sum(less.astype(I32), axis=1)
    return rank, place


def plan(pivots, y, z):
    r = y * Z + z
    t = jnp.arange(NB, dtype=I32)
    piv0, piv1 = pivots[0], pivots[1]
    meet = piv1[:, None] == piv0[None, :]
    src1 = jnp.where(jnp.any(meet, 1), jnp.sum(jnp.where(meet, t[None, :], 0), 1), piv1)
    src = (piv0, src1)
    in_home = piv0[:, None] == NB + t[None, :]
    moved = piv0[:, None] == piv1[None, :]
    dst0 = jnp.where(
        jnp.any(in_home, 1),
        jnp.sum(jnp.where(in_home, piv1[None, :], 0), 1),
        jnp.where(jnp.any(moved, 1), NB + jnp.sum(jnp.where(moved, t[None, :], 0), 1), piv0),
    )
    taken = (NB + t)[:, None] == piv0[None, :]
    dst1 = jnp.where(jnp.any(taken, 1), jnp.sum(jnp.where(taken, t[None, :], 0), 1), piv1)
    dst = (dst0, dst1)

    k_rank, k_place, k_key = [], [], []
    h_rank, h_place, h_key = [], [], []
    for h in range(2):
        own = h * NB + t
        stay = src[h] == own
        key = jnp.where(stay, -1, src[h] // NB)
        rank, place = ranks(key)
        k_key.append(key), k_rank.append(rank), k_place.append(place)
        away = dst[h] >= 2 * NB
        hkey = jnp.where(stay, -1, jnp.where(away, dst[h] // NB, 32))
        rank, place = ranks(hkey)
        h_key.append(hkey), h_rank.append(rank), h_place.append(place)
    over = jnp.zeros((), jnp.bool_)
    for h in range(2):
        over = over | jnp.any((k_key[h] >= 0) & (k_rank[h] >= CAP))
        over = over | jnp.any((h_key[h] >= 0) & (h_key[h] < 32) & (h_rank[h] >= CAP))
        over = over | jnp.any((h_key[h] < 0) & (h_rank[h] >= 4 * KEEP))

    def spot(place):
        return (place % 4) * 128 + place // 4

    mine = z % 2
    pick = lambda pair: jnp.where(mine == 0, pair[0], pair[1])
    home_spot = spot(pick(h_place))
    home_list = jnp.sum(jnp.where(home_spot[None, :] == t[:, None], t[None, :], 0), 1)
    e = jnp.arange(4 * SLOTS, dtype=I32)
    give = []
    for h in range(2):
        code = jnp.where(k_key[h] == r, (k_place[h] % 4) * SLOTS + k_rank[h] // 4, -1)
        code = jnp.where(k_rank[h] < CAP, code, -1)
        give.append(jnp.sum(jnp.where(code[None, :] == e[:, None], (src[h] % NB)[None, :], 0), 1))
    give_list = jnp.concatenate(give)
    place, key, rank = pick(k_place), pick(k_key), pick(k_rank)
    code = jnp.where(key < 0, -1, jnp.minimum(key * SLOTS + rank // 4, 32 * SLOTS - 1))
    i = jnp.arange(128, dtype=I32) * 4 + y
    slice_list = jnp.sum(jnp.where(place[None, :] == i[:, None], code[None, :], 0), 1)
    place, key, rank = pick(h_place), pick(h_key), pick(h_rank)
    ok = (place % 4 == y) & (key >= 0) & (key < 32) & (rank < CAP)
    code = jnp.where(ok, key * SLOTS + rank // 4, -1)
    e = jnp.arange(32 * SLOTS, dtype=I32)
    away_list = jnp.sum(jnp.where(code[None, :] == e[:, None], (place // 4)[None, :], 0), 1)
    e = jnp.arange(CAP, dtype=I32)
    to_row, from_y = [], []
    for h in range(2):
        hit = ((h_key[h] == r)[None, :]) & (h_rank[h][None, :] == e[:, None])
        to_row.append(jnp.sum(jnp.where(hit, (dst[h] % NB + 1)[None, :], 0), 1) - 1)
        from_y.append(jnp.sum(jnp.where(hit, (h_place[h] % 4)[None, :], 0), 1))
    to_row, from_y = jnp.concatenate(to_row), jnp.concatenate(from_y)
    hot = [jnp.broadcast_to(spot(k_place[h])[:, None], (NB, LANES)) for h in range(2)]
    return home_list, give_list, slice_list, away_list, to_row, from_y, hot, over


VMEM = pl.BlockSpec(memory_space=pltpu.VMEM)
SMEM = pl.BlockSpec(memory_space=pltpu.SMEM)


def call(kernel, name, out_shape, in_specs, mib, us, scratch=(), alias=None, out_specs=None):
    return pl.pallas_call(
        kernel,
        out_shape=out_shape,
        in_specs=in_specs,
        out_specs=[VMEM] * len(out_shape) if out_specs is None else out_specs,
        scratch_shapes=list(scratch),
        input_output_aliases=alias or {},
        compiler_params=pltpu.CompilerParams(vmem_limit_bytes=mib << 20),
        cost_estimate=pl.CostEstimate(flops=0, bytes_accessed=us * 3_000_000, transcendentals=0),
        name=name,
    )


def shaped(*shape, dtype=F32):
    return jax.ShapeDtypeStruct(shape, dtype)


def pack_kernel(home_ref, give_ref, x_ref, h_ref, rest_ref, g_ref):
    def give(n, _):
        row = give_ref[n] * SUB
        h, y, s = n // (4 * SLOTS), (n // SLOTS) % 4, n % SLOTS
        for k in range(4):
            g_ref[pl.ds(((y * 8 + 2 * k + h) * SLOTS + s) * 4, 4), :] = x_ref[pl.ds(row + k, 4, stride=4), :]
        return 0

    def keep(n, _):
        y, i = n // KEEP, n % KEEP
        row = home_ref[y * 128 + i] * SUB
        for k in range(4):
            h_ref[pl.ds((y * 4 + k) * WAVE + i * 4, 4), :] = x_ref[pl.ds(row + k, 4, stride=4), :]
        return 0

    def rest(n, _):
        y, i = n // REST, n % REST
        row = home_ref[y * 128 + KEEP + i] * SUB
        for k in range(4):
            h_ref[pl.ds((y * 4 + k) * WAVE + 4 * KEEP + i, 1), :] = x_ref[pl.ds(row + k, 1), :]
            rest_ref[pl.ds(((y * 4 + k) * REST + i) * 3, 3), :] = x_ref[pl.ds(row + 4 + k, 3, stride=4), :]
        return 0

    lax.fori_loop(0, 8 * SLOTS, give, 0, unroll=8)
    lax.fori_loop(0, 4 * KEEP, keep, 0, unroll=8)
    lax.fori_loop(0, 4 * REST, rest, 0, unroll=8)


def pack(home_list, give_list, x):
    out = [shaped(16 * WAVE, LANES), shaped(16 * REST * 3, LANES), shaped(32 * SLOTS * 4, LANES)]
    return call(pack_kernel, "pack", out, [SMEM, SMEM, VMEM], 24, 8)(home_list, give_list, x)


def slice_kernel(slice_ref, hs_ref, recv_ref, s_ref):
    def one(i, _):
        code = slice_ref[i]
        theirs = recv_ref[pl.ds(jnp.maximum(code, 0) * 4, 4), :]
        here = hs_ref[pl.ds(jnp.minimum(i, KEEP - 1) * 4, 4), :]
        s_ref[pl.ds(i, 4, stride=128), :] = jnp.where(code < 0, here, theirs)
        return 0

    lax.fori_loop(0, 128, one, 0, unroll=8)


def make_slice(slice_list, hs, recv):
    return call(slice_kernel, "pivot_slice", [shaped(512, LANES)], [SMEM, VMEM, VMEM], 16, 2)(slice_list, hs, recv)[0]


def away_kernel(away_ref, keep_ref, d_ref):
    def away(n, _):
        i = away_ref[n]
        d_ref[pl.ds(n, 1), :] = keep_ref[pl.ds(jnp.where(i < KEEP, i * 4, i + 3 * KEEP), 1), :]
        return 0

    lax.fori_loop(0, 32 * SLOTS, away, 0, unroll=8)


def make_away(away_list, keep):
    out = [shaped(32 * SLOTS, LANES)]
    return call(away_kernel, "away_first", out, [SMEM, VMEM], 16, 1)(away_list, keep)[0]


def away_rest_kernel(away_ref, keep_ref, rest_ref, d_ref):
    def away(n, _):
        i = away_ref[n]
        a = keep_ref[pl.ds(jnp.minimum(i, KEEP - 1) * 4 + 1, 3), :]
        b = rest_ref[pl.ds(jnp.maximum(i - KEEP, 0) * 3, 3), :]
        d_ref[pl.ds(n * 3, 3), :] = jnp.where(i < KEEP, a, b)
        return 0

    lax.fori_loop(0, 32 * SLOTS, away, 0, unroll=8)


def make_away_rest(away_list, keep, rest):
    out = [shaped(32 * SLOTS * 3, LANES)]
    return call(away_rest_kernel, "away_rest", out, [SMEM, VMEM, VMEM], 16, 2)(away_list, keep, rest)[0]


def patch_kernel(row_ref, y_ref, x_ref, first_ref, rest_ref, o_ref):
    o_ref[...] = x_ref[...]

    def one(n, _):
        row, y = row_ref[n], y_ref[n]
        h, s = n // CAP, (n % CAP) // 4

        @pl.when(row >= 0)
        def _():
            o_ref[pl.ds(row * SUB, 4), :] = first_ref[pl.ds((y * 8 + h) * SLOTS + s, 4, stride=2 * SLOTS), :]
            for k in range(4):
                piece = rest_ref[pl.ds(((y * 8 + 2 * k + h) * SLOTS + s) * 3, 3), :]
                o_ref[pl.ds(row * SUB + 4 + k, 3, stride=4), :] = piece

        return 0

    lax.fori_loop(0, 2 * CAP, one, 0)


def patch(to_row, from_y, x, first, rest):
    out = [shaped(NB * SUB, LANES)]
    return call(patch_kernel, "patch_rows", out, [SMEM] * 2 + [VMEM] * 3, 24, 4)(to_row, from_y, x, first, rest)[0]


def split(v):
    hi = v.astype(jnp.bfloat16)
    return hi, (v - hi.astype(F32)).astype(jnp.bfloat16)


def dot3(a, b):
    dot = functools.partial(jnp.dot, preferred_element_type=F32)
    return dot(a[0], b[0]) + dot(a[0], b[1]) + dot(a[1], b[0])


OFF_X = (0, -1, 1, 2)


def factor_kernel(
    info_ref, row_ref, y_ref, own_ref, swap_ref, late_ref, late_swap, piece_ref, piece_swap,
    inv0_ref, inv1_ref, spot0_ref, spot1_ref,
    m_ref, sp_ref, a0, a1, u01, p0, lin0, lin1,
):
    r, c, x, core = info_ref[4], info_ref[5], info_ref[6], info_ref[7]
    first = core == 0
    own, other = own_ref[...], swap_ref[...]
    lin0[...] = jnp.where(first, own, other)
    lin1[...] = jnp.where(first, other, own)

    def one(n, _):
        row, y = row_ref[n], y_ref[n]
        h, s = n // CAP, (n % CAP) // 4

        @pl.when(row >= 0)
        def _():
            at = pl.ds((y * 8 + h) * SLOTS + s, 4, stride=2 * SLOTS)
            own, other = late_ref[at, :], late_swap[at, :]
            lin0[pl.ds(row * 4, 4), :] = jnp.where(first, own, other)
            lin1[pl.ds(row * 4, 4), :] = jnp.where(first, other, own)

        return 0

    lax.fori_loop(0, 2 * CAP, one, 0)
    for j in range(4):
        cols = slice(j * 128, (j + 1) * 128)
        a0[:, cols] = lin0[pl.ds(j, NB, stride=4), :]
        a1[:, cols] = lin1[pl.ds(j, NB, stride=4), :]
    for m, dx in enumerate(OFF_X):
        for ref, cc in ((piece_ref, core), (piece_swap, 1 - core)):
            part = lax.rem(x + (dx + 4), 4) * 2 + cc
            for yy in range(4):
                rows = pl.ds(pl.multiple_of(yy * 128 + part * 16, 16), 16)
                for k in range(4):
                    cols = slice(k * 128, (k + 1) * 128)
                    u01[rows, cols] = ref[m, yy * 8 + 2 * k]
                    p0[rows, cols] = ref[m, yy * 8 + 2 * k + 1]

    dot = functools.partial(jnp.dot, preferred_element_type=F32)
    place = lax.broadcasted_iota(I32, (NB, NB), 1)
    hot0 = jnp.where(spot0_ref[:, :1] == place, 1.0, 0.0)
    hot1 = jnp.where(spot1_ref[:, :1] == place, 1.0, 0.0)
    inv0, inv1 = split(inv0_ref[...]), split(inv1_ref[...])

    def turned(inv, hot):
        hot = hot.astype(jnp.bfloat16)
        return tuple(dot(v, hot).astype(jnp.bfloat16) for v in inv)

    inv0p, inv1p = turned(inv0, hot0), turned(inv1, hot1)
    p0s = split(p0[...])

    @pl.when(r == 1)
    def _():
        at = hot1.astype(jnp.bfloat16)
        a0[...] = dot(at, p0s[0]) + dot(at, p0s[1])

    def put(at, v):
        hi, lo = split(v)
        m_ref[:NB, at : at + NB] = hi
        m_ref[NB:, at : at + NB] = lo

    l0 = dot3(split(a0[...]), inv0p)
    a1[...] = a1[...] - dot3(split(l0), split(u01[...]))
    l1 = dot3(split(a1[...]), inv1p)
    lp0 = dot3(p0s, inv0p)
    m0 = jnp.where(r == 1, l0, l0 - dot3(split(l1), split(lp0)))
    put(0, jnp.where(r == 0, -hot0, m0))
    put(NB, jnp.where(r == 0, 0.0, jnp.where(r == 1, -hot1, l1)))

    @pl.when(c == 0)
    def _():
        sp_ref[...] = dot3(split(a0[...]), inv0)

    @pl.when(c != 0)
    def _():
        sp_ref[...] = dot3(split(a1[...]), inv1)


def factors(info, to_row, from_y, *rest):
    out = [shaped(2 * NB, 2 * NB, dtype=jnp.bfloat16), shaped(NB, NB)]
    scratch = [pltpu.VMEM((NB, NB), F32)] * 4 + [pltpu.VMEM((NB * 4, LANES), F32)] * 2
    specs = [SMEM] * 3 + [VMEM] * len(rest)
    return call(factor_kernel, "factors", out, specs, 48, 12, scratch)(info, to_row, from_y, *rest)


OFF_Y = (0, -1, 1, 2)


def update_kernel(info_ref, x_ref, m_ref, sp_ref, u_ref, o_ref, uh, ul):
    i = pl.program_id(0)
    y, home, special = info_ref[0], info_ref[2], info_ref[3]
    x2, o2 = x_ref.reshape(NB * 8, LANES), o_ref.reshape(NB * 8, LANES)
    for m, dy in enumerate(OFF_Y):
        at = lax.rem(y + (dy + 4), 4) * 128
        for zz in range(4):
            rows = pl.ds(pl.multiple_of((zz % 2) * 512 + at, 128), 128)
            cols = slice(zz // 2 * 128, zz // 2 * 128 + 128)
            uh[rows, cols], ul[rows, cols] = split(u_ref[zz, m, 0])
    dot = functools.partial(jnp.dot, preferred_element_type=F32)
    both = dot(m_ref[...], uh[...])
    acc = both[:NB] + both[NB:] + dot(m_ref[:NB, :], ul[...])
    for s in range(2):
        j = 2 * lax.rem(i, 4) + s
        base = x2[pl.ds(j, NB, stride=8), :]
        new = jnp.where(home > 0, 0.0, base) - acc[:, s * 128 : (s + 1) * 128]
        put = sp_ref[:, pl.ds(pl.multiple_of(lax.rem(j, 4) * 128, 128), 128)]
        o2[pl.ds(j, NB, stride=8), :] = jnp.where((special > 0) & (i < 2), put, new)


def update(info, x, m, special, rows):
    half = pl.BlockSpec((NB, 8, LANES), lambda i: (0, i // 4, 0))
    whole = pl.BlockSpec((2 * NB, 2 * NB), lambda i: (0, 0))
    tile = pl.BlockSpec((4, 4, 1, 128, 128), lambda i: (i % 2, 0, i // 2, 0, 0))
    return pl.pallas_call(
        update_kernel,
        out_shape=shaped(NB, SUB, LANES),
        grid=(8,),
        in_specs=[SMEM, half, whole, pl.BlockSpec((NB, NB), lambda i: (0, 0)), tile],
        out_specs=half,
        scratch_shapes=[pltpu.VMEM((1024, 256), jnp.bfloat16)] * 2,
        compiler_params=pltpu.CompilerParams(vmem_limit_bytes=60 << 20),
        cost_estimate=pl.CostEstimate(flops=0, bytes_accessed=30_000_000, transcendentals=0),
        name="update",
    )(info, x, m, special, rows)


def join_kernel(count, *refs):
    parts, outs = refs[:-count], refs[-count:]
    each = len(parts) // count
    for n, ref in enumerate(parts):
        outs[n // each][n % each] = ref[...]


def join(parts, count=1):
    out = [shaped(len(parts) // count, *parts[0].shape)] * count
    return call(functools.partial(join_kernel, count), "join", out, [VMEM] * len(parts), 16, 1)(*parts)


def shift(v, axis, step):
    n = {"y": Y, "z": Z, "x": X, "core": CORE}[axis]
    return lax.ppermute(v, axis, [(i, (i + step) % n) for i in range(n)])


def tie(*values):
    return lax.optimization_barrier(values)


def scatter_y(blocks):
    go = lambda b: lax.ppermute(blocks[b], ROW, [(h, b * Z + h) for h in range(2)])
    return go(2), go(1), go(3)


def scatter_z(block):
    out = []
    for k in (2, 1, 3):
        pairs = [(i * Z + h, i * Z + 2 * k + h) for i in range(Y) for h in range(2)]
        out.append(lax.ppermute(block[k], ROW, pairs))
    return out


def body(matrix, pivots, inverses):
    y, z = lax.axis_index("y"), lax.axis_index("z")
    x, core = lax.axis_index("x"), lax.axis_index("core")
    r = y * Z + z
    c = x * CORE + core
    work = matrix.reshape(NB * SUB, LANES)
    panel = work.reshape(NB, SUB, LANES)[:, :4].reshape(NB * 4, LANES)
    panel = jnp.where(x == 0, panel, 0.0)
    home_list, give_list, slice_list, away_list, to_row, from_y, hot, over = plan(pivots, y, z)
    is_special = ((c == 0) & (r >= 1)) | ((c == 1) & (r >= 2))
    info = jnp.stack([y, z, (r < 2).astype(I32), is_special.astype(I32), r, c, x, core])
    inv0, inv1 = inverses[0], inverses[1]

    keep, rest, send = pack(home_list, give_list, work)
    keep, rest = keep.reshape(4, 4, WAVE, LANES), rest.reshape(4, 4, REST * 3, LANES)
    keep_y = scatter_y(keep)
    recv = lax.all_to_all(send.reshape(32, 4 * SLOTS, LANES), ROW, 0, 0)
    keep = jnp.where(y == 0, keep[0], sum(keep_y))
    keep_z = scatter_z(keep)
    keep, panel, to_row, from_y, spot0, spot1, *keep_z = tie(keep, panel, to_row, from_y, *hot, *keep_z)
    keep = jnp.where(z < 2, keep[0], sum(keep_z))
    panel = lax.psum(panel, "x")
    mine = make_slice(slice_list, keep, recv.reshape(-1, LANES)).reshape(4, 128, LANES)

    parts = [shift(mine, "y", n) for n in (1, -1, 2)]
    away = make_away(away_list, keep)
    away, rest, *parts = tie(away, rest, *parts)
    rows = lax.all_gather(join([mine] + parts)[0], "z", axis=0)

    recv_first = lax.all_to_all(away.reshape(32, SLOTS, LANES), ROW, 0, 0)
    rest_y = scatter_y(rest)
    piece = lax.all_to_all(mine[0].reshape(8, 16, LANES), COL, 0, 0)
    piece, recv_first, *rest_y = tie(piece, recv_first, *rest_y)
    rest = jnp.where(y == 0, rest[0], sum(rest_y))
    rest_z = scatter_z(rest)
    piece = lax.dynamic_slice_in_dim(piece, 1 - z % 2, 1, 0)
    piece = lax.all_to_all(jnp.broadcast_to(piece, (32, 16, LANES)), ROW, 0, 0)
    late = recv_first.reshape(-1, LANES)
    late_x = [lax.ppermute(late, "x", [(0, b)]) for b in (2, 1, 3)]
    piece, la, lb, lc, *rest_z = tie(piece, *late_x, *rest_z)
    late = jnp.where(x == 0, late, la + lb + lc)
    late_swap = shift(late, "core", 1)
    pieces = [shift(piece, "x", n) for n in (1, -1, 2)]
    swap = shift(panel, "core", 1)
    rest = jnp.where(z < 2, rest[0], sum(rest_z))
    away = make_away_rest(away_list, keep, rest)
    recv_rest = lax.all_to_all(away.reshape(32, SLOTS * 3, LANES), ROW, 0, 0)
    late_swap, swap, *pieces = tie(late_swap, swap, *pieces)
    piece = join([piece] + pieces)[0]
    piece_swap = shift(piece, "core", 1)
    m, special = factors(
        info, to_row, from_y, panel, swap, late, late_swap, piece, piece_swap, inv0, inv1, spot0, spot1,
    )
    m, special, recv_rest = tie(m, special, recv_rest)
    base = patch(to_row, from_y, work, recv_first.reshape(-1, LANES), recv_rest.reshape(-1, LANES))
    out = update(info, base.reshape(NB, SUB, LANES), m, special, rows)
    out = out.reshape(NB * SUB, LANES)
    out = lax.cond(over, lambda o: general(work, pivots, inverses), lambda o: o, out)
    return out.reshape(matrix.shape)


def solution(mesh):
    grid = Mesh(mesh.devices.reshape(Y, Z, X, CORE), ("y", "z", "x", "core"))
    placed = (P(None, ROW, None, None, COL, None), P(), P())
    return jax.shard_map(
        body,
        mesh=grid,
        in_specs=placed,
        out_specs=P(None, ROW, None, None, COL, None),
        check_vma=False,
    )
```

```python
import functools

import jax
import jax.numpy as jnp
from jax import lax
from jax.experimental import pallas as pl
from jax.experimental.pallas import tpu as pltpu
from jax.sharding import Mesh, PartitionSpec as P

Y, Z, X, CORE = 4, 8, 4, 2
NB = 512
LANES = 128
SUB = 16
SLOTS = 8
CAP = 4 * SLOTS
KEEP = 32
REST = 128 - KEEP
WAVE = 4 * KEEP + REST
ROW = ("y", "z")
COL = ("x", "core")
HIGHEST = lax.Precision.HIGHEST
F32 = jnp.float32
I32 = jnp.int32


def from_root(x, axis, root):
    mine = lax.axis_index(axis) == root
    return lax.psum(jnp.where(mine, x, jnp.zeros_like(x)), axis)


def general(work, pivots, inverses):
    row_index = lax.axis_index(ROW)
    col_index = lax.axis_index(COL)
    work = work.reshape(NB, SUB * LANES)
    row_ids = row_index * NB + jnp.arange(NB, dtype=I32)
    col_ids = (
        (jnp.arange(4, dtype=I32)[:, None] * 8 + col_index) * NB
        + jnp.arange(NB, dtype=I32)[None, :]
    ).reshape(-1)
    for panel in range(2):
        after_row = (panel + 1) * NB
        targets = pivots[panel]
        held = targets // NB == row_index
        local_row = targets % NB
        picked = jnp.where(held[:, None], jnp.take(work, local_row, axis=0), 0.0)
        u_rows = lax.psum(picked, ROW)
        displaced = from_root(work, ROW, panel)
        dest_row = jnp.where(held, local_row, NB)
        work = work.at[dest_row].set(displaced, mode="drop")
        work = jnp.where(row_index == panel, u_rows, work)
        panel_cols = work[:, :NB]
        product = jnp.dot(panel_cols, inverses[panel], precision=HIGHEST)
        l_cols = from_root(product, COL, panel)
        below_mask = (row_ids >= after_row)[:, None]
        work = work.at[:, :NB].set(
            jnp.where(below_mask & (col_index == panel), l_cols, panel_cols)
        )
        update = jnp.dot(l_cols, u_rows, precision=HIGHEST)
        trail_mask = below_mask & (col_ids >= after_row)[None, :]
        work = jnp.where(trail_mask, work - update, work)
    return work.reshape(NB * SUB, LANES)


def ranks(key):
    t = jnp.arange(NB, dtype=I32)
    same = (key[:, None] == key[None, :]) & (t[None, :] < t[:, None])
    less = key[None, :] < key[:, None]
    rank = jnp.sum(same.astype(I32), axis=1)
    place = rank + jnp.sum(less.astype(I32), axis=1)
    return rank, place


def plan(pivots, y, z):
    r = y * Z + z
    t = jnp.arange(NB, dtype=I32)
    piv0, piv1 = pivots[0], pivots[1]
    meet = piv1[:, None] == piv0[None, :]
    src1 = jnp.where(jnp.any(meet, 1), jnp.sum(jnp.where(meet, t[None, :], 0), 1), piv1)
    src = (piv0, src1)
    in_home = piv0[:, None] == NB + t[None, :]
    moved = piv0[:, None] == piv1[None, :]
    dst0 = jnp.where(
        jnp.any(in_home, 1),
        jnp.sum(jnp.where(in_home, piv1[None, :], 0), 1),
        jnp.where(jnp.any(moved, 1), NB + jnp.sum(jnp.where(moved, t[None, :], 0), 1), piv0),
    )
    taken = (NB + t)[:, None] == piv0[None, :]
    dst1 = jnp.where(jnp.any(taken, 1), jnp.sum(jnp.where(taken, t[None, :], 0), 1), piv1)
    dst = (dst0, dst1)

    k_rank, k_place, k_key = [], [], []
    h_rank, h_place, h_key = [], [], []
    for h in range(2):
        own = h * NB + t
        stay = src[h] == own
        key = jnp.where(stay, -1, src[h] // NB)
        rank, place = ranks(key)
        k_key.append(key), k_rank.append(rank), k_place.append(place)
        away = dst[h] >= 2 * NB
        hkey = jnp.where(stay, -1, jnp.where(away, dst[h] // NB, 32))
        rank, place = ranks(hkey)
        h_key.append(hkey), h_rank.append(rank), h_place.append(place)
    over = jnp.zeros((), jnp.bool_)
    for h in range(2):
        over = over | jnp.any((k_key[h] >= 0) & (k_rank[h] >= CAP))
        over = over | jnp.any((h_key[h] >= 0) & (h_key[h] < 32) & (h_rank[h] >= CAP))
        over = over | jnp.any((h_key[h] < 0) & (h_rank[h] >= 4 * KEEP))

    def spot(place):
        return (place % 4) * 128 + place // 4

    mine = z % 2
    pick = lambda pair: jnp.where(mine == 0, pair[0], pair[1])
    home_spot = spot(pick(h_place))
    home_list = jnp.sum(jnp.where(home_spot[None, :] == t[:, None], t[None, :], 0), 1)
    e = jnp.arange(4 * SLOTS, dtype=I32)
    give = []
    for h in range(2):
        code = jnp.where(k_key[h] == r, (k_place[h] % 4) * SLOTS + k_rank[h] // 4, -1)
        code = jnp.where(k_rank[h] < CAP, code, -1)
        give.append(jnp.sum(jnp.where(code[None, :] == e[:, None], (src[h] % NB)[None, :], 0), 1))
    give_list = jnp.concatenate(give)
    place, key, rank = pick(k_place), pick(k_key), pick(k_rank)
    code = jnp.where(key < 0, -1, jnp.minimum(key * SLOTS + rank // 4, 32 * SLOTS - 1))
    i = jnp.arange(128, dtype=I32) * 4 + y
    slice_list = jnp.sum(jnp.where(place[None, :] == i[:, None], code[None, :], 0), 1)
    place, key, rank = pick(h_place), pick(h_key), pick(h_rank)
    ok = (place % 4 == y) & (key >= 0) & (key < 32) & (rank < CAP)
    code = jnp.where(ok, key * SLOTS + rank // 4, -1)
    e = jnp.arange(32 * SLOTS, dtype=I32)
    away_list = jnp.sum(jnp.where(code[None, :] == e[:, None], (place // 4)[None, :], 0), 1)
    e = jnp.arange(CAP, dtype=I32)
    to_row, from_y = [], []
    for h in range(2):
        hit = ((h_key[h] == r)[None, :]) & (h_rank[h][None, :] == e[:, None])
        to_row.append(jnp.sum(jnp.where(hit, (dst[h] % NB + 1)[None, :], 0), 1) - 1)
        from_y.append(jnp.sum(jnp.where(hit, (h_place[h] % 4)[None, :], 0), 1))
    to_row, from_y = jnp.concatenate(to_row), jnp.concatenate(from_y)
    hot = [jnp.broadcast_to(spot(k_place[h])[:, None], (NB, LANES)) for h in range(2)]
    return home_list, give_list, slice_list, away_list, to_row, from_y, hot, over


VMEM = pl.BlockSpec(memory_space=pltpu.VMEM)
SMEM = pl.BlockSpec(memory_space=pltpu.SMEM)


def call(kernel, name, out_shape, in_specs, mib, us, scratch=(), alias=None, out_specs=None):
    return pl.pallas_call(
        kernel,
        out_shape=out_shape,
        in_specs=in_specs,
        out_specs=[VMEM] * len(out_shape) if out_specs is None else out_specs,
        scratch_shapes=list(scratch),
        input_output_aliases=alias or {},
        compiler_params=pltpu.CompilerParams(vmem_limit_bytes=mib << 20),
        cost_estimate=pl.CostEstimate(flops=0, bytes_accessed=us * 3_000_000, transcendentals=0),
        name=name,
    )


def shaped(*shape, dtype=F32):
    return jax.ShapeDtypeStruct(shape, dtype)


def pack_kernel(home_ref, give_ref, x_ref, h_ref, rest_ref, g_ref):
    def give(n, _):
        row = give_ref[n] * SUB
        h, y, s = n // (4 * SLOTS), (n // SLOTS) % 4, n % SLOTS
        for k in range(4):
            g_ref[pl.ds(((y * 8 + 2 * k + h) * SLOTS + s) * 4, 4), :] = x_ref[pl.ds(row + k, 4, stride=4), :]
        return 0

    def keep(n, _):
        y, i = n // KEEP, n % KEEP
        row = home_ref[y * 128 + i] * SUB
        for k in range(4):
            h_ref[pl.ds((y * 4 + k) * WAVE + i * 4, 4), :] = x_ref[pl.ds(row + k, 4, stride=4), :]
        return 0

    def rest(n, _):
        y, i = n // REST, n % REST
        row = home_ref[y * 128 + KEEP + i] * SUB
        for k in range(4):
            h_ref[pl.ds((y * 4 + k) * WAVE + 4 * KEEP + i, 1), :] = x_ref[pl.ds(row + k, 1), :]
            rest_ref[pl.ds(((y * 4 + k) * REST + i) * 3, 3), :] = x_ref[pl.ds(row + 4 + k, 3, stride=4), :]
        return 0

    lax.fori_loop(0, 8 * SLOTS, give, 0, unroll=8)
    lax.fori_loop(0, 4 * KEEP, keep, 0, unroll=8)
    lax.fori_loop(0, 4 * REST, rest, 0, unroll=8)


def pack(home_list, give_list, x):
    out = [shaped(16 * WAVE, LANES), shaped(16 * REST * 3, LANES), shaped(32 * SLOTS * 4, LANES)]
    return call(pack_kernel, "pack", out, [SMEM, SMEM, VMEM], 24, 8)(home_list, give_list, x)


def slice_kernel(slice_ref, hs_ref, recv_ref, s_ref):
    def one(i, _):
        code = slice_ref[i]
        theirs = recv_ref[pl.ds(jnp.maximum(code, 0) * 4, 4), :]
        here = hs_ref[pl.ds(jnp.minimum(i, KEEP - 1) * 4, 4), :]
        s_ref[pl.ds(i, 4, stride=128), :] = jnp.where(code < 0, here, theirs)
        return 0

    lax.fori_loop(0, 128, one, 0, unroll=8)


def make_slice(slice_list, hs, recv):
    return call(slice_kernel, "pivot_slice", [shaped(512, LANES)], [SMEM, VMEM, VMEM], 16, 2)(slice_list, hs, recv)[0]


def away_kernel(away_ref, keep_ref, d_ref):
    def away(n, _):
        i = away_ref[n]
        d_ref[pl.ds(n, 1), :] = keep_ref[pl.ds(jnp.where(i < KEEP, i * 4, i + 3 * KEEP), 1), :]
        return 0

    lax.fori_loop(0, 32 * SLOTS, away, 0, unroll=8)


def make_away(away_list, keep):
    out = [shaped(32 * SLOTS, LANES)]
    return call(away_kernel, "away_first", out, [SMEM, VMEM], 16, 1)(away_list, keep)[0]


def away_rest_kernel(away_ref, keep_ref, rest_ref, d_ref):
    def away(n, _):
        i = away_ref[n]
        a = keep_ref[pl.ds(jnp.minimum(i, KEEP - 1) * 4 + 1, 3), :]
        b = rest_ref[pl.ds(jnp.maximum(i - KEEP, 0) * 3, 3), :]
        d_ref[pl.ds(n * 3, 3), :] = jnp.where(i < KEEP, a, b)
        return 0

    lax.fori_loop(0, 32 * SLOTS, away, 0, unroll=8)


def make_away_rest(away_list, keep, rest):
    out = [shaped(32 * SLOTS * 3, LANES)]
    return call(away_rest_kernel, "away_rest", out, [SMEM, VMEM, VMEM], 16, 2)(away_list, keep, rest)[0]


def patch_kernel(row_ref, y_ref, x_ref, first_ref, rest_ref, o_ref):
    o_ref[...] = x_ref[...]

    def one(n, _):
        row, y = row_ref[n], y_ref[n]
        h, s = n // CAP, (n % CAP) // 4

        @pl.when(row >= 0)
        def _():
            o_ref[pl.ds(row * SUB, 4), :] = first_ref[pl.ds((y * 8 + h) * SLOTS + s, 4, stride=2 * SLOTS), :]
            for k in range(4):
                piece = rest_ref[pl.ds(((y * 8 + 2 * k + h) * SLOTS + s) * 3, 3), :]
                o_ref[pl.ds(row * SUB + 4 + k, 3, stride=4), :] = piece

        return 0

    lax.fori_loop(0, 2 * CAP, one, 0)


def patch(to_row, from_y, x, first, rest):
    out = [shaped(NB * SUB, LANES)]
    return call(patch_kernel, "patch_rows", out, [SMEM] * 2 + [VMEM] * 3, 24, 4)(to_row, from_y, x, first, rest)[0]


def split(v):
    hi = v.astype(jnp.bfloat16)
    return hi, (v - hi.astype(F32)).astype(jnp.bfloat16)


def dot3(a, b):
    dot = functools.partial(jnp.dot, preferred_element_type=F32)
    return dot(a[0], b[0]) + dot(a[0], b[1]) + dot(a[1], b[0])


OFF_X = (0, -1, 1, 2)


def factor_kernel(
    info_ref, row_ref, y_ref, own_ref, swap_ref, late_ref, late_swap, piece_ref, piece_swap,
    inv_ref, spot0_ref, spot1_ref,
    m_ref, sp_ref, a0, a1, u01, p0, lin0, lin1,
):
    r, c, x, core = info_ref[4], info_ref[5], info_ref[6], info_ref[7]
    first = core == 0
    own, other = own_ref[...], swap_ref[...]
    lin0[...] = jnp.where(first, own, other)
    lin1[...] = jnp.where(first, other, own)

    def one(n, _):
        row, y = row_ref[n], y_ref[n]
        h, s = n // CAP, (n % CAP) // 4

        @pl.when(row >= 0)
        def _():
            at = pl.ds((y * 8 + h) * SLOTS + s, 4, stride=2 * SLOTS)
            own, other = late_ref[at, :], late_swap[at, :]
            lin0[pl.ds(row * 4, 4), :] = jnp.where(first, own, other)
            lin1[pl.ds(row * 4, 4), :] = jnp.where(first, other, own)

        return 0

    lax.fori_loop(0, 2 * CAP, one, 0)
    for j in range(4):
        cols = slice(j * 128, (j + 1) * 128)
        a0[:, cols] = lin0[pl.ds(j, NB, stride=4), :]
        a1[:, cols] = lin1[pl.ds(j, NB, stride=4), :]
    for m, dx in enumerate(OFF_X):
        for ref, cc in ((piece_ref, core), (piece_swap, 1 - core)):
            part = lax.rem(x + (dx + 4), 4) * 2 + cc
            for yy in range(4):
                rows = pl.ds(pl.multiple_of(yy * 128 + part * 16, 16), 16)
                for k in range(4):
                    cols = slice(k * 128, (k + 1) * 128)
                    u01[rows, cols] = ref[m, yy * 8 + 2 * k]
                    p0[rows, cols] = ref[m, yy * 8 + 2 * k + 1]

    dot = functools.partial(jnp.dot, preferred_element_type=F32)
    place = lax.broadcasted_iota(I32, (NB, NB), 1)
    hot0 = jnp.where(spot0_ref[:, :1] == place, 1.0, 0.0)
    hot1 = jnp.where(spot1_ref[:, :1] == place, 1.0, 0.0)
    inv0, inv1 = split(inv_ref[0]), split(inv_ref[1])

    def turned(inv, hot):
        hot = hot.astype(jnp.bfloat16)
        return tuple(dot(v, hot).astype(jnp.bfloat16) for v in inv)

    inv0p, inv1p = turned(inv0, hot0), turned(inv1, hot1)
    p0s = split(p0[...])

    @pl.when(r == 1)
    def _():
        at = hot1.astype(jnp.bfloat16)
        a0[...] = dot(at, p0s[0]) + dot(at, p0s[1])

    def put(at, v):
        hi, lo = split(v)
        m_ref[:NB, at : at + NB] = hi
        m_ref[NB:, at : at + NB] = lo

    l0 = dot3(split(a0[...]), inv0p)
    a1[...] = a1[...] - dot3(split(l0), split(u01[...]))
    l1 = dot3(split(a1[...]), inv1p)
    lp0 = dot3(p0s, inv0p)
    m0 = jnp.where(r == 1, l0, l0 - dot3(split(l1), split(lp0)))
    put(0, jnp.where(r == 0, -hot0, m0))
    put(NB, jnp.where(r == 0, 0.0, jnp.where(r == 1, -hot1, l1)))

    @pl.when(c == 0)
    def _():
        sp_ref[...] = dot3(split(a0[...]), inv0)

    @pl.when(c != 0)
    def _():
        sp_ref[...] = dot3(split(a1[...]), inv1)


def factors(info, to_row, from_y, *rest):
    out = [shaped(2 * NB, 2 * NB, dtype=jnp.bfloat16), shaped(NB, NB)]
    scratch = [pltpu.VMEM((NB, NB), F32)] * 4 + [pltpu.VMEM((NB * 4, LANES), F32)] * 2
    specs = [SMEM] * 3 + [VMEM] * len(rest)
    return call(factor_kernel, "factors", out, specs, 48, 12, scratch)(info, to_row, from_y, *rest)


OFF_Y = (0, -1, 1, 2)


def update_kernel(info_ref, x_ref, m_ref, sp_ref, u_ref, o_ref, uh, ul):
    i = pl.program_id(0)
    y, home, special = info_ref[0], info_ref[2], info_ref[3]
    x2, o2 = x_ref.reshape(NB * 8, LANES), o_ref.reshape(NB * 8, LANES)
    for m, dy in enumerate(OFF_Y):
        at = lax.rem(y + (dy + 4), 4) * 128
        for zz in range(4):
            rows = pl.ds(pl.multiple_of((zz % 2) * 512 + at, 128), 128)
            cols = slice(zz // 2 * 128, zz // 2 * 128 + 128)
            uh[rows, cols], ul[rows, cols] = split(u_ref[zz, m, 0])
    dot = functools.partial(jnp.dot, preferred_element_type=F32)
    both = dot(m_ref[...], uh[...])
    acc = both[:NB] + both[NB:] + dot(m_ref[:NB, :], ul[...])
    for s in range(2):
        j = 2 * lax.rem(i, 4) + s
        base = x2[pl.ds(j, NB, stride=8), :]
        new = jnp.where(home > 0, 0.0, base) - acc[:, s * 128 : (s + 1) * 128]
        put = sp_ref[:, pl.ds(pl.multiple_of(lax.rem(j, 4) * 128, 128), 128)]
        o2[pl.ds(j, NB, stride=8), :] = jnp.where((special > 0) & (i < 2), put, new)


def update(info, x, m, special, rows):
    half = pl.BlockSpec((NB, 8, LANES), lambda i: (0, i // 4, 0))
    whole = pl.BlockSpec((2 * NB, 2 * NB), lambda i: (0, 0))
    tile = pl.BlockSpec((4, 4, 1, 128, 128), lambda i: (i % 2, 0, i // 2, 0, 0))
    return pl.pallas_call(
        update_kernel,
        out_shape=shaped(NB, SUB, LANES),
        grid=(8,),
        in_specs=[SMEM, half, whole, pl.BlockSpec((NB, NB), lambda i: (0, 0)), tile],
        out_specs=half,
        scratch_shapes=[pltpu.VMEM((1024, 256), jnp.bfloat16)] * 2,
        compiler_params=pltpu.CompilerParams(vmem_limit_bytes=60 << 20),
        cost_estimate=pl.CostEstimate(flops=0, bytes_accessed=30_000_000, transcendentals=0),
        name="update",
    )(info, x, m, special, rows)


def join_kernel(count, *refs):
    parts, outs = refs[:-count], refs[-count:]
    each = len(parts) // count
    for n, ref in enumerate(parts):
        outs[n // each][n % each] = ref[...]


def join(parts, count=1):
    out = [shaped(len(parts) // count, *parts[0].shape)] * count
    return call(functools.partial(join_kernel, count), "join", out, [VMEM] * len(parts), 16, 1)(*parts)


def shift(v, axis, step):
    n = {"y": Y, "z": Z, "x": X, "core": CORE}[axis]
    return lax.ppermute(v, axis, [(i, (i + step) % n) for i in range(n)])


def tie(*values):
    return lax.optimization_barrier(values)


def scatter_y(blocks):
    go = lambda b: lax.ppermute(blocks[b], ROW, [(h, b * Z + h) for h in range(2)])
    return go(2), go(1), go(3)


def scatter_z(block):
    out = []
    for k in (2, 1, 3):
        pairs = [(i * Z + h, i * Z + 2 * k + h) for i in range(Y) for h in range(2)]
        out.append(lax.ppermute(block[k], ROW, pairs))
    return out


def body(matrix, pivots, inverses):
    y, z = lax.axis_index("y"), lax.axis_index("z")
    x, core = lax.axis_index("x"), lax.axis_index("core")
    r = y * Z + z
    c = x * CORE + core
    work = matrix.reshape(NB * SUB, LANES)
    panel = work.reshape(NB, SUB, LANES)[:, :4].reshape(NB * 4, LANES)
    panel = jnp.where(x == 0, panel, 0.0)
    home_list, give_list, slice_list, away_list, to_row, from_y, hot, over = plan(pivots, y, z)
    is_special = ((c == 0) & (r >= 1)) | ((c == 1) & (r >= 2))
    info = jnp.stack([y, z, (r < 2).astype(I32), is_special.astype(I32), r, c, x, core])

    keep, rest, send = pack(home_list, give_list, work)
    keep, rest = keep.reshape(4, 4, WAVE, LANES), rest.reshape(4, 4, REST * 3, LANES)
    keep_y = scatter_y(keep)
    recv = lax.all_to_all(send.reshape(32, 4 * SLOTS, LANES), ROW, 0, 0)
    keep = jnp.where(y == 0, keep[0], sum(keep_y))
    keep_z = scatter_z(keep)
    keep, panel, spot0, spot1, *keep_z = tie(keep, panel, *hot, *keep_z)
    keep = jnp.where(z < 2, keep[0], sum(keep_z))
    panel = lax.psum(panel, "x")
    mine = make_slice(slice_list, keep, recv.reshape(-1, LANES)).reshape(4, 128, LANES)

    parts = [shift(mine, "y", n) for n in (1, -1, 2)]
    away = make_away(away_list, keep)
    away, rest, *parts = tie(away, rest, *parts)
    rows = lax.all_gather(join([mine] + parts)[0], "z", axis=0)

    recv_first = lax.all_to_all(away.reshape(32, SLOTS, LANES), ROW, 0, 0)
    rest_y = scatter_y(rest)
    piece = lax.all_to_all(mine[0].reshape(8, 16, LANES), COL, 0, 0)
    over = over.astype(I32)
    piece, recv_first, over, to_row, from_y, *rest_y = tie(piece, recv_first, over, to_row, from_y, *rest_y)
    rest = jnp.where(y == 0, rest[0], sum(rest_y))
    rest_z = scatter_z(rest)
    piece = lax.dynamic_slice_in_dim(piece, 1 - z % 2, 1, 0)
    piece = lax.all_to_all(jnp.broadcast_to(piece, (32, 16, LANES)), ROW, 0, 0)
    late = recv_first.reshape(-1, LANES)
    late_x = [lax.ppermute(late, "x", [(0, b)]) for b in (2, 1, 3)]
    piece, la, lb, lc, *rest_z = tie(piece, *late_x, *rest_z)
    late = jnp.where(x == 0, late, la + lb + lc)
    late_swap = shift(late, "core", 1)
    pieces = [shift(piece, "x", n) for n in (1, -1, 2)]
    swap = shift(panel, "core", 1)
    rest = jnp.where(z < 2, rest[0], sum(rest_z))
    away = make_away_rest(away_list, keep, rest)
    recv_rest = lax.all_to_all(away.reshape(32, SLOTS * 3, LANES), ROW, 0, 0)
    recv_rest, late_swap, swap, *pieces = tie(recv_rest, late_swap, swap, *pieces)
    piece = join([piece] + pieces)[0]
    piece_swap = shift(piece, "core", 1)
    base = patch(to_row, from_y, work, recv_first.reshape(-1, LANES), recv_rest.reshape(-1, LANES))
    m, special = factors(
        info, to_row, from_y, panel, swap, late, late_swap, piece, piece_swap, inverses, spot0, spot1,
    )
    out = update(info, base.reshape(NB, SUB, LANES), m, special, rows)
    out = out.reshape(NB * SUB, LANES)
    out = lax.cond(over > 0, lambda o: general(work, pivots, inverses), lambda o: o, out)
    return out.reshape(matrix.shape)


def solution(mesh):
    grid = Mesh(mesh.devices.reshape(Y, Z, X, CORE), ("y", "z", "x", "core"))
    placed = (P(None, ROW, None, None, COL, None), P(), P())
    return jax.shard_map(
        body,
        mesh=grid,
        in_specs=placed,
        out_specs=P(None, ROW, None, None, COL, None),
        check_vma=False,
    )
```
